32 devices in a mesh: gx: 4 (over y, core), gy: 8 (over z, x).
Axes of the slice: x: 2, y: 2, z: 4, core: 2. Of those that a mesh axis runs over, the one named last changes fastest.
Arguments:
- positions: int32 [4, 8, 3, 49152], P('gx', 'gy'), may hold values from -16 to 271, as said below
- velocity: float32 [4, 8, 3, 49152], P('gx', 'gy'), may hold values from -6 to 6
- random_velocity: float32 [4, 8, 3, 49152], P('gx', 'gy'), may hold values from -6 to 6
- masses: float32 [4, 8, 49152], P('gx', 'gy'), may hold values from 0.25 to 4
- counts: int32 [4, 8], P('gx', 'gy'), may hold values from 12288 to 49152, as said below
- grid_shift: int32 [3], replicated, may hold values from 1 to 15
Outputs:
- new_velocity: float32 [4, 8, 3, 49152], P('gx', 'gy')
The draws below stay inside these ranges and needn't reach their ends.
Inputs may be any that keep to these rules, and one draw needn't show every extreme that they name: Rows 0 and 1 of positions lie in [-16, 272) and [-16, 272); row 2 lies in [0, 128). Slots at or past a device's count hold positions in the same ranges. The first counts[i, j] slots of device (i, j) hold its particles; at least one device holds 49152.
All inputs are finite; a program needn't handle non-finite values.
Results may differ from the reference program's by a relative error of at most 0.0003.
Values sent between devices are 32-bit elements; how exact they have to be, the bound alone decides.
No kernel may reach another device: no remote copies, remote signals or barrier semaphores. Data moves between devices by JAX's collectives and lax.ppermute only.
A program may use at most 64 MiB of HBM per device.

```python
import math
import jax
import jax.numpy as jnp
from jax import lax

CX = 16
CY = 16
NZ = 8
SKIN = 1
SUB = 16
SLOTS = 49152
NXC = 64
NYC = 128
N_GX = 4
N_GY = 8


def draw_positions(key, part):
    subkeys = jax.random.split(jax.random.fold_in(key, 11), 5)
    array_shape = (N_GX, N_GY, SLOTS)
    inner_x = jax.random.randint(subkeys[0], array_shape, 0, CX * SUB, dtype=jnp.int32)
    moved_x = jax.random.randint(subkeys[1], array_shape, -SKIN * SUB, SKIN * SUB, dtype=jnp.int32)
    inner_y = jax.random.randint(subkeys[2], array_shape, 0, CY * SUB, dtype=jnp.int32)
    moved_y = jax.random.randint(subkeys[3], array_shape, -SKIN * SUB, SKIN * SUB, dtype=jnp.int32)
    layer_z = jax.random.randint(subkeys[4], array_shape, 0, NZ * SUB, dtype=jnp.int32)
    return jnp.stack([inner_x + moved_x, inner_y + moved_y, layer_z], axis=2).astype(jnp.int32)


def draw_counts(key, part):
    subkeys = jax.random.split(jax.random.fold_in(key, 23), 2)
    drawn = jax.random.randint(subkeys[0], (N_GX * N_GY,), SLOTS // 4, SLOTS // 2 + 1, dtype=jnp.int32)
    fullest = jax.random.randint(subkeys[1], (), 0, N_GX * N_GY, dtype=jnp.int32)
    device_index = jnp.arange(N_GX * N_GY, dtype=jnp.int32)
    return jnp.where(device_index == fullest, SLOTS, drawn).reshape(N_GX, N_GY).astype(jnp.int32)


def shard_levels(rng, extent, cuts, low, largest):
    loudness, own = 1.0, jax.random.fold_in(rng, 6)
    for position, parts in cuts:
        steps = jnp.exp(jax.random.uniform(jax.random.fold_in(own, position), (parts,), jnp.float32, low / len(cuts), largest / len(cuts)))
        loudness = loudness * jnp.repeat(steps, extent[position] // parts).reshape([-1 if axis == position else 1 for axis in range(len(extent))])
    return loudness


def gaussian(key, dims, deviation, reach, cuts=(), kind=jnp.bfloat16):
    factor_of = shard_levels(key, dims, cuts, -0.22, 0.18) if cuts else 1.0
    result = jax.random.normal(key, dims, jnp.float32) * deviation * factor_of
    return jnp.minimum(jnp.maximum(result, -reach), reach).astype(kind)


def setup_inputs(seed: int = 0) -> dict:
    keys = jax.random.split(jax.random.key(seed), 7)
    return {
        "positions": draw_positions(jax.random.fold_in(keys[6], 71), 0),
        "velocity": gaussian(keys[1], (N_GX, N_GY, 3, SLOTS), 1.0, 6.0, ((0, 4), (1, 8)), jnp.float32),
        "random_velocity": gaussian(keys[2], (N_GX, N_GY, 3, SLOTS), 1.0, 6.0, ((0, 4), (1, 8)), jnp.float32),
        "masses": jnp.clip(jnp.exp(math.log(4.0) - 2.7725887 * jax.random.uniform(keys[3], (N_GX, N_GY, SLOTS), jnp.float32) ** shard_levels(keys[3], (N_GX, N_GY, SLOTS), ((0, 4), (1, 8)), -0.2, 0.2)), 0.25, 4.0),
        "counts": draw_counts(jax.random.fold_in(keys[6], 71), 0),
        "grid_shift": jax.random.randint(keys[5], (3,), 1, SUB).astype(jnp.int32),
    }


def reference(positions, velocity, random_velocity, masses, counts, grid_shift):
    total_cells = NXC * NYC * NZ
    column_index = jnp.arange(N_GY, dtype=jnp.int32)[:, None]
    slot_index = jnp.arange(SLOTS, dtype=jnp.int32)[None, :]

    def locate(row_index):
        places = positions[row_index]
        cell_x = jnp.floor_divide(row_index * (CX * SUB) + places[:, 0] + grid_shift[0], SUB) % NXC
        cell_y = jnp.floor_divide(column_index * (CY * SUB) + places[:, 1] + grid_shift[1], SUB) % NYC
        cell_z = jnp.floor_divide(places[:, 2] + grid_shift[2], SUB) % NZ
        flat_cell = ((cell_x * NYC + cell_y) * NZ + cell_z).astype(jnp.int32)
        alive_mask = slot_index < counts[row_index][:, None]
        return flat_cell, alive_mask

    def accumulate(totals, row_index):
        flat_cell, alive_mask = locate(row_index)
        weight = jnp.where(alive_mask, masses[row_index], jnp.float32(0.0))
        moving = velocity[row_index]
        thermal = random_velocity[row_index]
        fields = jnp.concatenate([weight[:, None] * moving, weight[:, None], weight[:, None] * thermal], axis=1)
        fields = jnp.transpose(fields, (1, 0, 2)).reshape(7, -1)
        cell_rows = flat_cell.reshape(-1)

        def sum_field(field_row):
            return jax.ops.segment_sum(field_row, cell_rows, num_segments=total_cells)

        return totals + jax.vmap(sum_field)(fields), None

    totals, unused = lax.scan(accumulate, jnp.zeros((7, total_cells), jnp.float32), jnp.arange(N_GX, dtype=jnp.int32))
    momentum = totals[0:3]
    mass_total = totals[3]
    random_total = totals[4:7]
    filled = mass_total > 0
    drift = jnp.where(filled, (momentum - random_total) / jnp.where(filled, mass_total, jnp.float32(1.0)), jnp.float32(0.0))

    def emit(row_index):
        flat_cell, alive_mask = locate(row_index)
        gathered = jnp.transpose(jnp.take(drift, flat_cell, axis=1), (1, 0, 2))
        return jnp.where(alive_mask[:, None, :], gathered + random_velocity[row_index], jnp.float32(0.0))

    return lax.map(emit, jnp.arange(N_GX, dtype=jnp.int32))
```

```python
import functools
import jax, jax.numpy as jnp
from jax import lax
from jax.experimental import pallas as pl
from jax.sharding import PartitionSpec as P
from jax.experimental.pallas import tpu as pltpu

CX = CY = 16; NZ = 8; SKIN = 1; SUB = 16
EX = CX + 2*SKIN + 1; EY = CY + 2*SKIN + 1
NB = EY*NZ
NAP = 20
CHUNK = 8192

def bcast_rows(row, n):
    return jnp.broadcast_to(row, (n, row.shape[-1]))

def indices(pos, sx, sy, sz):
    ax = ((pos[0:1] + sx) >> 4) + SKIN
    by = ((pos[1:2] + sy) >> 4) + SKIN
    bz = ((pos[2:3] + sz) >> 4) & (NZ-1)
    return ax, by*NZ + bz

def scatter_kernel(shift, count, pos_h, vel_h, rnd_h, mass_h, out, pos_v, vel_v, rnd_v, mass_v, sems):
    slots = pos_h.shape[1]
    n = count[0, 0]
    live = (n + (CHUNK-1)) // CHUNK
    sx, sy, sz = shift[0], shift[1], shift[2]
    def copies(i):
        s = pl.ds(pl.multiple_of(i*CHUNK, CHUNK), CHUNK)
        return [pltpu.make_async_copy(h.at[:, s], v.at[:, s], sems.at[i]) for h, v in
                ((pos_h, pos_v), (vel_h, vel_v), (rnd_h, rnd_v), (mass_h, mass_v))]
    def start(i, c):
        for x in copies(i): x.start()
        return c
    lax.fori_loop(0, live, start, 0)
    out[...] = jnp.zeros_like(out)
    row16 = lax.broadcasted_iota(jnp.int32, (16, CHUNK), 0)
    def body(i, c):
        for x in copies(i): x.wait()
        s = pl.ds(pl.multiple_of(i*CHUNK, CHUNK), CHUNK)
        a, b = indices(pos_v[:, s], sx, sy, sz)
        lane = lax.broadcasted_iota(jnp.int32, (1, CHUNK), 1) + i*CHUNK
        w = jnp.where(lane < n, mass_v[:, s], 0.0)
        d = (vel_v[:, s] - rnd_v[:, s]) * w
        x4 = jnp.concatenate([d, w], axis=0)
        x8 = jnp.concatenate([x4, x4], axis=0)
        hi = x8.astype(jnp.bfloat16).astype(jnp.float32)
        row8 = lax.broadcasted_iota(jnp.int32, (8, CHUNK), 0)
        v8 = jnp.where(row8 < 4, hi, x8 - hi)
        v16 = jnp.concatenate([v8, v8], axis=0).astype(jnp.bfloat16)
        a16 = (bcast_rows(a, 16) - (row16 >> 3)).astype(jnp.float32).astype(jnp.bfloat16)
        b16 = (bcast_rows(b, 16) - row16).astype(jnp.float32).astype(jnp.bfloat16)
        zero = jnp.zeros((), jnp.bfloat16)
        lhs = jnp.concatenate([jnp.where(a16 == jnp.bfloat16(2*t), v16, zero) for t in range(NAP//2)], axis=0)
        one = jnp.ones((16, CHUNK), jnp.bfloat16)
        rhs = jnp.concatenate([jnp.where(b16 == jnp.bfloat16(16*t), one, zero) for t in range(10)], axis=0)
        out[...] += lax.dot_general(lhs, rhs, (((1,), (1,)), ((), ())), preferred_element_type=jnp.float32)
        return c
    lax.fori_loop(0, live, body, 0)

def scatter(shift, count, pos, vel, rnd, mass):
    slots = pos.shape[1]
    hbm = pl.BlockSpec(memory_space=pltpu.HBM)
    sm = pl.BlockSpec(memory_space=pltpu.SMEM)
    return pl.pallas_call(
        scatter_kernel,
        out_shape=jax.ShapeDtypeStruct((160, 160), jnp.float32),
        in_specs=[sm, sm, hbm, hbm, hbm, hbm],
        out_specs=pl.BlockSpec(memory_space=pltpu.VMEM),
        scratch_shapes=[pltpu.VMEM((3, slots), jnp.int32), pltpu.VMEM((3, slots), jnp.float32), pltpu.VMEM((3, slots), jnp.float32),
                        pltpu.VMEM((1, slots), jnp.float32), pltpu.SemaphoreType.DMA((slots//CHUNK,))],
        compiler_params=pltpu.CompilerParams(vmem_limit_bytes=40*1024*1024),
        name="scatter",
    )(shift, count, pos, vel, rnd, mass)

def gather_kernel(shift, count, table, pos_h, rnd_h, out_h, pos_v, rnd_v, out_v, sems, osems):
    slots = pos_h.shape[1]
    n = count[0, 0]
    live = (n + (CHUNK-1)) // CHUNK
    sx, sy, sz = shift[0], shift[1], shift[2]
    def copies(i):
        s = pl.ds(pl.multiple_of(i*CHUNK, CHUNK), CHUNK)
        return [pltpu.make_async_copy(h.at[:, s], v.at[:, s], sems.at[i]) for h, v in
                ((pos_h, pos_v), (rnd_h, rnd_v))]
    def ocopy(i):
        s = pl.ds(pl.multiple_of(i*CHUNK, CHUNK), CHUNK)
        return pltpu.make_async_copy(out_v.at[:, s], out_h.at[:, s], osems.at[i])
    def start(i, c):
        for x in copies(i): x.start()
        return c
    lax.fori_loop(0, live, start, 0)
    def dead(i, c):
        s = pl.ds(pl.multiple_of(i*CHUNK, CHUNK), CHUNK)
        out_v[:, s] = jnp.zeros((3, CHUNK), jnp.float32)
        ocopy(i).start()
        return c
    lax.fori_loop(live, slots//CHUNK, dead, 0)
    t8 = table[...].reshape(NAP, 8, table.shape[1])
    t8 = t8 + pltpu.roll(t8, 4, 1)
    mass = t8[:, 3:4]
    filled = mass > 0
    t8 = jnp.where(filled, t8 / jnp.where(filled, mass, 1.0), 0.0).reshape(NAP // 2, 2, 8, table.shape[1])
    rowt = lax.broadcasted_iota(jnp.int32, (1, 8, table.shape[1]), 1)
    t32 = jnp.where(rowt < 4, t8[:, 0], t8[:, 1]).reshape(NAP * 4, table.shape[1])
    hi = t32.astype(jnp.bfloat16)
    lo = (t32 - hi.astype(jnp.float32)).astype(jnp.bfloat16)
    row8 = lax.broadcasted_iota(jnp.int32, (8, CHUNK), 0)
    row16 = lax.broadcasted_iota(jnp.int32, (16, CHUNK), 0)
    def body(i, c):
        for x in copies(i): x.wait()
        s = pl.ds(pl.multiple_of(i*CHUNK, CHUNK), CHUNK)
        a, b = indices(pos_v[:, s], sx, sy, sz)
        zero = jnp.zeros((), jnp.bfloat16)
        b16 = (bcast_rows(b, 16) - row16).astype(jnp.float32).astype(jnp.bfloat16)
        one = jnp.ones((16, CHUNK), jnp.bfloat16)
        rhs = jnp.concatenate([jnp.where(b16 == jnp.bfloat16(16*t), one, zero) for t in range(10)], axis=0)
        ph = jnp.dot(hi, rhs, preferred_element_type=jnp.float32)
        plo = jnp.dot(lo, rhs, preferred_element_type=jnp.float32)
        a8 = bcast_rows(a, 8) - (row8 >> 2)
        acc = jnp.zeros((8, CHUNK), jnp.float32)
        acl = jnp.zeros((8, CHUNK), jnp.float32)
        for t in range(NAP//2):
            m = a8 == 2*t
            acc = jnp.where(m, ph[8*t:8*t+8], acc)
            acl = jnp.where(m, plo[8*t:8*t+8], acl)
        acc = acc + acl
        picked = acc[0:3] + acc[4:7]
        lane = lax.broadcasted_iota(jnp.int32, (3, CHUNK), 1) + i*CHUNK
        out_v[:, s] = jnp.where(lane < n, picked + rnd_v[:, s], 0.0)
        ocopy(i).start()
        return c
    lax.fori_loop(0, live, body, 0)
    def fin(i, c):
        ocopy(i).wait()
        return c
    lax.fori_loop(0, slots//CHUNK, fin, 0)

def gather(shift, count, table, pos, rnd):
    slots = pos.shape[1]
    hbm = pl.BlockSpec(memory_space=pltpu.HBM)
    sm = pl.BlockSpec(memory_space=pltpu.SMEM)
    return pl.pallas_call(
        gather_kernel,
        out_shape=jax.ShapeDtypeStruct((3, slots), jnp.float32),
        in_specs=[sm, sm, pl.BlockSpec(memory_space=pltpu.VMEM), hbm, hbm],
        out_specs=hbm,
        scratch_shapes=[pltpu.VMEM((3, slots), jnp.int32), pltpu.VMEM((3, slots), jnp.float32), pltpu.VMEM((3, slots), jnp.float32),
                        pltpu.SemaphoreType.DMA((slots//CHUNK,)), pltpu.SemaphoreType.DMA((slots//CHUNK,))],
        compiler_params=pltpu.CompilerParams(vmem_limit_bytes=40*1024*1024),
        name="gather",
    )(shift, count, table, pos, rnd)


def shifted(x, axis, step):
    n = lax.axis_size(axis)
    return lax.ppermute(x, axis, [(i, (i + step) % n) for i in range(n)])


def on_device(positions, velocity, random_velocity, masses, counts, grid_shift):
    pos, vel, rnd, mass = positions[0, 0], velocity[0, 0], random_velocity[0, 0], masses[0]
    acc = scatter(grid_shift, counts, pos, vel, rnd, mass)
    lo, hi = 24, 128
    left = shifted(acc[hi:hi + lo], "gx", 1)
    right = shifted(acc[0:lo], "gx", -1)
    acc = jnp.concatenate([acc[0:lo] + left, acc[lo:hi], acc[hi:hi + lo] + right, acc[hi + lo:]], axis=0)
    left = shifted(acc[:, hi:hi + lo], "gy", 1)
    right = shifted(acc[:, 0:lo], "gy", -1)
    acc = jnp.concatenate([acc[:, 0:lo] + left, acc[:, lo:hi], acc[:, hi:hi + lo] + right, acc[:, hi + lo:]], axis=1)
    out = gather(grid_shift, counts, acc, pos, rnd)
    return out[None, None]


def solution(mesh):
    return jax.shard_map(
        on_device, mesh=mesh,
        in_specs=(P("gx", "gy", None, None), P("gx", "gy", None, None), P("gx", "gy", None, None), P("gx", "gy", None), P("gx", "gy"), P()),
        out_specs=P("gx", "gy", None, None), check_vma=False)
```

```python
import functools
import jax, jax.numpy as jnp
from jax import lax
from jax.experimental import pallas as pl
from jax.experimental.pallas import tpu as pltpu
from jax.sharding import PartitionSpec as P

CX = CY = 16; NZ = 8; SKIN = 1; SUB = 16
EX = CX + 2*SKIN + 1; EY = CY + 2*SKIN + 1
LANES = 128
CH = 64
RIM = 2 * SKIN + 1
BF = jnp.bfloat16
SCATTER_VMEM = 55060*1024

def up(x, m): return (x + m - 1) // m * m
NB = up(EY*NZ, 16)
NA = up(EX, 2)

def row_iota(shape): return lax.broadcasted_iota(jnp.int32, shape, len(shape) - 2)

def spread(ref, base, count, sublanes):
    return jnp.concatenate([jnp.broadcast_to(ref[pl.ds(base + g, 1), :], (sublanes, LANES)) for g in range(count)], axis=1)

def place(pos_v, s, shift, kind=jnp.float32):
    a = ((pos_v[0, s] + shift[0]) >> 4) + SKIN
    b = (((pos_v[1, s] + shift[1]) >> 4) + SKIN) * NZ + (((pos_v[2, s] + shift[2]) >> 4) & (NZ - 1))
    return a.astype(kind), b.astype(kind)

def load_shift(shift_h, shift, sem):
    copy = pltpu.make_async_copy(shift_h, shift, sem)
    copy.start()
    return copy

def scatter_kernel(shift_h, count, pos_h, vel_h, rnd_h, mass_h, out, pos_v, vel_v, rnd_v, mass_v, val_v, a_v, b_v, shift, ssem, sems):
    shift_copy = load_shift(shift_h, shift, ssem)
    per = CH * LANES
    def copies(i):
        s = pl.ds(pl.multiple_of(i*CH, CH), CH)
        return [pltpu.make_async_copy(h.at[:, s], v.at[:, s], sems.at[i]) for h, v in
                ((pos_h, pos_v), (vel_h, vel_v), (rnd_h, rnd_v), (mass_h, mass_v))]
    def start(i, c):
        for x in copies(i): x.start()
        return c
    start(0, 0)
    out[...] = jnp.zeros_like(out)
    shift_copy.wait()
    moved = [shift[0, f] for f in range(3)]
    n = count[0, 0]
    live = (n + (per - 1)) // per
    lax.fori_loop(1, live, start, 0)
    slot = lax.broadcasted_iota(jnp.int32, (CH, LANES), 0) * LANES + lax.broadcasted_iota(jnp.int32, (CH, LANES), 1)
    def body(i, c):
        for x in copies(i): x.wait()
        base = pl.multiple_of(i*CH, CH)
        s = pl.ds(base, CH)
        a_v[...], b_v[...] = place(pos_v, s, moved)
        w = jnp.where(slot + i*per < n, mass_v[0, s], 0.0)
        fields = [(vel_v[f, s] - rnd_v[f, s]) * w for f in range(3)] + [w]
        for f, x in enumerate(fields):
            hi = x.astype(BF).astype(jnp.float32)
            val_v[pl.ds(f, CH, stride=8), :] = hi
            val_v[pl.ds(f + 4, CH, stride=8), :] = x - hi
        b16 = spread(b_v, 0, CH, 16).astype(BF)
        rhs = hot_tiles(b16, range(NB // 16))
        a16 = spread(a_v, 0, CH, 16).astype(BF)
        width = CH * LANES
        rel = a16 - (row_iota((16, width)) >> 3).astype(jnp.float32).astype(BF)
        v8 = [val_v[pl.ds(8*g, 8), :] for g in range(CH)]
        v16 = jnp.concatenate([jnp.concatenate([x, x], axis=0) for x in v8], axis=1).astype(BF)
        zero = jnp.zeros((16, width), BF)
        lhs = jnp.concatenate([jnp.where(rel == BF(2*t), v16, zero) for t in range(NA // 2)], axis=0)
        out[...] += lax.dot_general(lhs, rhs, (((1,), (1,)), ((), ())), preferred_element_type=jnp.float32)
        return c
    lax.fori_loop(0, live, body, 0)
    lane = lax.broadcasted_iota(jnp.int32, (1, NB), 1)
    out[KEPT:KEPT + 1, :] = jnp.where(lane == 0, moved[0], jnp.where(lane == 1, moved[1], moved[2])).astype(jnp.float32)

def scatter(shift, count, pos, vel, rnd, mass):
    rows = pos.shape[1]
    hbm = pl.BlockSpec(memory_space=pl.ANY)
    sm = pl.BlockSpec(memory_space=pltpu.SMEM)
    vm = pl.BlockSpec(memory_space=pltpu.VMEM)
    f32 = jnp.float32
    return pl.pallas_call(
        scatter_kernel,
        out_shape=jax.ShapeDtypeStruct((NA*8, NB), f32),
        in_specs=[hbm, sm, hbm, hbm, hbm, hbm],
        out_specs=vm,
        scratch_shapes=[pltpu.VMEM((3, rows, LANES), jnp.int32), pltpu.VMEM((3, rows, LANES), f32), pltpu.VMEM((3, rows, LANES), f32),
                        pltpu.VMEM((1, rows, LANES), f32), pltpu.VMEM((CH * 8, LANES), f32), pltpu.VMEM((CH, LANES), f32), pltpu.VMEM((CH, LANES), f32),
                        pltpu.SMEM(shift.shape, jnp.int32), pltpu.SemaphoreType.DMA(()), pltpu.SemaphoreType.DMA((rows // CH,))],
        compiler_params=pltpu.CompilerParams(vmem_limit_bytes=SCATTER_VMEM),
        name="scatter",
    )(shift, count, pos, vel, rnd, mass)

SB = 4
LO = RIM * NZ
HI = CY * NZ
MID = (LO // 16 * 16, HI)
RK = 2 * 2 * LO
GCH = 64
KEPT = EX * 8

def hot_tiles(b16, tiles):
    width = b16.shape[1]
    rel = b16 - row_iota((16, width)).astype(jnp.float32).astype(BF)
    one, zero = jnp.ones((16, width), BF), jnp.zeros((16, width), BF)
    return jnp.concatenate([jnp.where(rel == BF(16*t), one, zero) for t in tiles], axis=0)

def drifts(sums):
    t8 = sums + pltpu.roll(sums, 4, 1)
    mass = t8[:, 3:4]
    filled = mass > 0
    t8 = jnp.where(filled, t8 / jnp.where(filled, mass, 1.0), 0.0)
    hi = t8.astype(BF).astype(jnp.float32)
    return jnp.where(row_iota((1,) + t8.shape[1:]) < 3, hi, pltpu.roll(t8 - hi, 3, 1))

def pick(table, hot, a8, out_v, k, owner):
    p = jnp.dot(table, hot, preferred_element_type=jnp.float32)
    acc = [jnp.zeros(a8.shape, jnp.float32)] * 3
    rel = [a8 - o for o in owner]
    for t in range(table.shape[0] // 8):
        acc[t % 3] = jnp.where(rel[t % 3] == float(4 * (t // 3)), p[8*t:8*t+8], acc[t % 3])
    for g in range(SB):
        for q in range(3):
            out_v[pl.ds((k + g)*24 + 8*q, 8), :] = acc[q][:, g*LANES:(g+1)*LANES]

def picked(out_v, f):
    return sum([out_v[pl.ds(3*u + f, GCH, stride=24), :] for u in range(8)])

def owners():
    return [((row_iota((8, SB*LANES)) + 8*c) // 6).astype(jnp.float32) for c in range(3)]

def slots_at(i):
    cells = (GCH, LANES)
    return i*GCH*LANES + lax.broadcasted_iota(jnp.int32, cells, 0) * LANES + lax.broadcasted_iota(jnp.int32, cells, 1)

def split(rows):
    return max(2 * rows // GCH // 3, 1)

def kept_shift(sums):
    return [sums[KEPT:KEPT + 1, f:f + 1].astype(jnp.int32) for f in range(3)]

def fill_table(tab_v, t8):
    tab_v[...] = jnp.zeros_like(tab_v)
    for x in range(tab_v.shape[0] // 6):
        tab_v[pl.ds(6*x, 6), :] = t8[x, 0:6]
    return tab_v[...].astype(BF)

def middle_kernel(count, sums, pos_v, rnd_v, base, tab_v, pick_v, a_v, b_v):
    per = GCH * LANES
    lane = lax.broadcasted_iota(jnp.int32, (1, 1, MID[1]), 2)
    t8 = jnp.where(lane < LO, 0.0, drifts(sums[:, :MID[1]].reshape(NA, 8, MID[1])))
    table = fill_table(tab_v, t8)[:, MID[0]:]
    owner = owners()
    shift = kept_shift(sums)
    n = count[0, 0]
    def body(i, c):
        s = pl.ds(pl.multiple_of(i*GCH, GCH), GCH)
        a, b = place(pos_v, s, shift, jnp.int32)
        a_v[...], b_v[...] = a.astype(jnp.float32), b.astype(jnp.float32)
        for k in range(0, GCH, SB):
            hot = hot_tiles(spread(b_v, k, SB, 16).astype(BF), range(MID[0] // 16, MID[1] // 16))
            pick(table, hot, spread(a_v, k, SB, 8), pick_v, k, owner)
        alive = slots_at(i) < n
        for f in range(3):
            base[f, s] = jnp.where(alive, picked(pick_v, f) + rnd_v[f, s], 0.0)
        r = jnp.where(b < LO, b, b - (HI - LO)) + (a & 1) * (2 * LO)
        base[3, s] = (a >> 1).astype(jnp.float32)
        base[4, s] = jnp.where(((b < LO) | (b >= HI)) & alive, r, -1).astype(jnp.float32)
        return c
    lax.fori_loop(0, jnp.minimum((n + (per - 1)) // per, base.shape[1] // GCH), body, 0)

def middle(count, sums, pos, rnd):
    rows = rnd.shape[1]
    part = split(rows) * GCH
    sm = pl.BlockSpec(memory_space=pltpu.SMEM)
    vm = pl.BlockSpec(memory_space=pltpu.VMEM)
    f32 = jnp.float32
    return pl.pallas_call(
        middle_kernel,
        out_shape=jax.ShapeDtypeStruct((5, part, LANES), f32),
        in_specs=[sm, vm, vm, vm],
        out_specs=vm,
        scratch_shapes=[pltpu.VMEM((up(EX*6, 8), MID[1]), f32), pltpu.VMEM((GCH*24, LANES), f32), pltpu.VMEM((GCH, LANES), f32), pltpu.VMEM((GCH, LANES), f32)],
        compiler_params=pltpu.CompilerParams(vmem_limit_bytes=20*1024*1024),
        cost_estimate=pl.CostEstimate(flops=2 * rows * LANES * 128 * 128, bytes_accessed=rows * LANES * 36, transcendentals=0),
        name="middle",
    )(count, sums, pos, rnd)

def last_kernel(count, sums, right, left, base, pos_v, rnd_v, out_h, out_v, tab_v, full_v, pick_v, a_v, b_v, osems):
    rows = rnd_v.shape[1]
    per = GCH * LANES
    f32 = jnp.float32
    n = count[0, 0]
    live = (n + (per - 1)) // per
    early = jnp.minimum(live, base.shape[1] // GCH)
    def ocopy(i):
        s = pl.ds(pl.multiple_of(i*GCH, GCH), GCH)
        return pltpu.make_async_copy(out_v.at[:, s], out_h.at[:, s], osems.at[i])
    def dead(i, c):
        out_v[:, pl.ds(pl.multiple_of(i*GCH, GCH), GCH)] = jnp.zeros((3, GCH, LANES), f32)
        ocopy(i).start()
        return c
    lax.fori_loop(live, rows // GCH, dead, 0)
    low = sums[:, 0:LO] + left[...]
    high = sums[:, HI:HI + LO] + right[...]
    t8 = drifts(jnp.concatenate([low, high], axis=1).reshape(NA, 8, 2*LO)).reshape(NA // 2, 2, 8, 2*LO)
    table = fill_table(tab_v, jnp.concatenate([t8[:, 0], t8[:, 1]], axis=2))
    owner = owners()
    def body(i, c):
        s = pl.ds(pl.multiple_of(i*GCH, GCH), GCH)
        for k in range(0, GCH, SB):
            hot = hot_tiles(spread(base.at[4], i*GCH + k, SB, 16).astype(BF), range(RK // 16))
            pick(table, hot, spread(base.at[3], i*GCH + k, SB, 8), pick_v, k, owner)
        for f in range(3):
            out_v[f, s] = picked(pick_v, f) + base[f, s]
        ocopy(i).start()
        return c
    lax.fori_loop(0, early, body, 0)
    @pl.when(live > early)
    def _():
        both = jnp.concatenate([low, sums[:, LO:HI], high, sums[:, HI + LO:]], axis=1)
        table = fill_table(full_v, drifts(both.reshape(NA, 8, NB)))
        shift = kept_shift(sums)
        def body(i, c):
            s = pl.ds(pl.multiple_of(i*GCH, GCH), GCH)
            a_v[...], b_v[...] = place(pos_v, s, shift)
            for k in range(0, GCH, SB):
                hot = hot_tiles(spread(b_v, k, SB, 16).astype(BF), range(NB // 16))
                pick(table, hot, spread(a_v, k, SB, 8), pick_v, k, owner)
            alive = slots_at(i) < n
            for f in range(3):
                out_v[f, s] = jnp.where(alive, picked(pick_v, f) + rnd_v[f, s], 0.0)
            ocopy(i).start()
            return c
        lax.fori_loop(early, live, body, 0)
    def fin(i, c):
        ocopy(i).wait()
        return c
    lax.fori_loop(0, rows // GCH, fin, 0)

def last(count, sums, left, right, base, pos, rnd):
    rows = rnd.shape[1]
    hbm = pl.BlockSpec(memory_space=pl.ANY)
    sm = pl.BlockSpec(memory_space=pltpu.SMEM)
    vm = pl.BlockSpec(memory_space=pltpu.VMEM)
    f32 = jnp.float32
    return pl.pallas_call(
        last_kernel,
        out_shape=jax.ShapeDtypeStruct((3, rows, LANES), f32),
        in_specs=[sm, vm, vm, vm, vm, vm, vm],
        out_specs=hbm,
        scratch_shapes=[pltpu.VMEM((3, rows, LANES), f32), pltpu.VMEM((up(NA // 2 * 6, 8), RK), f32), pltpu.VMEM((up(EX*6, 8), NB), f32), pltpu.VMEM((GCH*24, LANES), f32),
                        pltpu.VMEM((GCH, LANES), f32), pltpu.VMEM((GCH, LANES), f32), pltpu.SemaphoreType.DMA((rows//GCH,))],
        compiler_params=pltpu.CompilerParams(vmem_limit_bytes=20*1024*1024),
        name="last",
    )(count, sums, right, left, base, pos, rnd)

def shifted(x, axis, step):
    n = lax.axis_size(axis)
    return lax.ppermute(x, axis, [(i, (i + step) % n) for i in range(n)])

def on_device(positions, velocity, random_velocity, masses, counts, grid_shift):
    dense = lambda x: x.reshape(x.shape[-2] if x.ndim == 4 else 1, x.shape[-1] // LANES, LANES)
    pos, vel, rnd, mass = map(dense, (positions, velocity, random_velocity, masses))
    shift = grid_shift.reshape(1, -1)
    acc = scatter(shift, counts, pos, vel, rnd, mass)
    lo, hi = RIM * 8, CX * 8
    left = shifted(acc[hi:hi + lo], "gx", 1)
    right = shifted(acc[0:lo], "gx", -1)
    acc = jnp.concatenate([acc[0:lo] + left, acc[lo:hi], acc[hi:hi + lo] + right, acc[hi + lo:]], axis=0)
    left = shifted(acc[:, HI:HI + LO], "gy", 1)
    right = shifted(acc[:, 0:LO], "gy", -1)
    base = middle(counts, acc, pos, rnd)
    out = last(counts, acc, left, right, base, pos, rnd)
    return out.reshape(random_velocity.shape)

def solution(mesh):
    return jax.shard_map(
        on_device, mesh=mesh,
        in_specs=(P("gx", "gy", None, None), P("gx", "gy", None, None), P("gx", "gy", None, None), P("gx", "gy", None), P("gx", "gy"), P()),
        out_specs=P("gx", "gy", None, None), check_vma=False)
```

```python
import functools
import jax, jax.numpy as jnp
from jax import lax
from jax.experimental import pallas as pl
from jax.experimental.pallas import tpu as pltpu
from jax.sharding import PartitionSpec as P

CX = CY = 16; NZ = 8; SKIN = 1; SUB = 16
EX = CX + 2*SKIN + 1; EY = CY + 2*SKIN + 1
LANES = 128
CH = 64
RIM = 2 * SKIN + 1
BF = jnp.bfloat16
SCATTER_VMEM = 55060*1024

def up(x, m): return (x + m - 1) // m * m
NB = up(EY*NZ, 16)
NA = up(EX, 2)

def row_iota(shape): return lax.broadcasted_iota(jnp.int32, shape, len(shape) - 2)

def spread(ref, base, count, sublanes):
    return jnp.concatenate([jnp.broadcast_to(ref[pl.ds(base + g, 1), :], (sublanes, LANES)) for g in range(count)], axis=1)

def place(pos_v, s, shift, kind=jnp.float32):
    a = ((pos_v[0, s] + shift[0]) >> 4)
    b = (((pos_v[1, s] + shift[1]) >> 4)) * NZ + (((pos_v[2, s] + shift[2]) >> 4) & (NZ - 1))
    return a.astype(kind), b.astype(kind)

def load_shift(shift_h, shift, sem):
    copy = pltpu.make_async_copy(shift_h, shift, sem)
    copy.start()
    return copy

def scatter_kernel(shift_h, count, pos_h, vel_h, rnd_h, mass_h, out, acc, pos_v, vel_v, rnd_v, mass_v, val_v, a_v, b_v, shift, ssem, sems):
    shift_copy = load_shift(shift_h, shift, ssem)
    per = CH * LANES
    def copies(i):
        s = pl.ds(pl.multiple_of(i*CH, CH), CH)
        return [pltpu.make_async_copy(h.at[:, s], v.at[:, s], sems.at[i]) for h, v in
                ((pos_h, pos_v), (vel_h, vel_v), (rnd_h, rnd_v), (mass_h, mass_v))]
    def start(i, c):
        for x in copies(i): x.start()
        return c
    start(0, 0)
    acc[...] = jnp.zeros_like(acc)
    shift_copy.wait()
    moved = [shift[0, f] for f in range(3)]
    n = count[0, 0]
    live = (n + (per - 1)) // per
    lax.fori_loop(1, live, start, 0)
    slot = lax.broadcasted_iota(jnp.int32, (CH, LANES), 0) * LANES + lax.broadcasted_iota(jnp.int32, (CH, LANES), 1)
    def body(i, c):
        for x in copies(i): x.wait()
        base = pl.multiple_of(i*CH, CH)
        s = pl.ds(base, CH)
        a_v[...], b_v[...] = place(pos_v, s, moved)
        w = jnp.where(slot + i*per < n, mass_v[0, s], 0.0)
        fields = [(vel_v[f, s] - rnd_v[f, s]) * w for f in range(3)] + [w]
        for f, x in enumerate(fields):
            hi = x.astype(BF).astype(jnp.float32)
            val_v[pl.ds(f, CH, stride=8), :] = hi
            val_v[pl.ds(f + 4, CH, stride=8), :] = x - hi
        b16 = spread(b_v, 0, CH, 16).astype(BF)
        rhs = hot_tiles(b16, range(NB // 16))
        a16 = spread(a_v, 0, CH, 16).astype(BF)
        width = CH * LANES
        rel = a16 - (row_iota((16, width)) >> 3).astype(jnp.float32).astype(BF)
        v8 = [val_v[pl.ds(8*g, 8), :] for g in range(CH)]
        v16 = jnp.concatenate([jnp.concatenate([x, x], axis=0) for x in v8], axis=1).astype(BF)
        zero = jnp.zeros((16, width), BF)
        lhs = jnp.concatenate([jnp.where(rel == BF(2*t), v16, zero) for t in range(NA // 2)], axis=0)
        acc[...] += lax.dot_general(lhs, rhs, (((1,), (1,)), ((), ())), preferred_element_type=jnp.float32)
        return c
    lax.fori_loop(0, live, body, 0)
    both = acc[...].reshape(NA // 2, 2, 8, NB)
    both = both + pltpu.roll(both.reshape(NA, 8, NB), 4, 1).reshape(both.shape)
    out[...] = jnp.where(row_iota((1, 8, NB)) < 4, both[:, 0], both[:, 1]).reshape(NA * 4, NB)

def scatter(shift, count, pos, vel, rnd, mass):
    rows = pos.shape[1]
    hbm = pl.BlockSpec(memory_space=pl.ANY)
    sm = pl.BlockSpec(memory_space=pltpu.SMEM)
    vm = pl.BlockSpec(memory_space=pltpu.VMEM)
    f32 = jnp.float32
    return pl.pallas_call(
        scatter_kernel,
        out_shape=jax.ShapeDtypeStruct((NA*4, NB), f32),
        in_specs=[hbm, sm, hbm, hbm, hbm, hbm],
        out_specs=vm,
        scratch_shapes=[pltpu.VMEM((NA*8, NB), f32), pltpu.VMEM((3, rows, LANES), jnp.int32), pltpu.VMEM((3, rows, LANES), f32), pltpu.VMEM((3, rows, LANES), f32),
                        pltpu.VMEM((1, rows, LANES), f32), pltpu.VMEM((CH * 8, LANES), f32), pltpu.VMEM((CH, LANES), f32), pltpu.VMEM((CH, LANES), f32),
                        pltpu.SMEM(shift.shape, jnp.int32), pltpu.SemaphoreType.DMA(()), pltpu.SemaphoreType.DMA((rows // CH,))],
        compiler_params=pltpu.CompilerParams(vmem_limit_bytes=SCATTER_VMEM),
        name="scatter",
    )(shift, count, pos, vel, rnd, mass)

SB = 4
LO = RIM * NZ
HI = CY * NZ
MID = (LO // 16 * 16, HI)
RK = 2 * 2 * LO
GCH = 64

def hot_tiles(b16, tiles):
    width = b16.shape[1]
    rel = b16 - row_iota((16, width)).astype(jnp.float32).astype(BF)
    one, zero = jnp.ones((16, width), BF), jnp.zeros((16, width), BF)
    return jnp.concatenate([jnp.where(rel == BF(16*t), one, zero) for t in tiles], axis=0)

def drifts(sums):
    row = row_iota((1,) + sums.shape[1:])
    mass = jnp.where(row < 4, sums[:, 3:4], sums[:, 7:8])
    filled = mass > 0
    drift = jnp.where(filled, sums / jnp.where(filled, mass, 1.0), 0.0)
    hi = drift.astype(BF).astype(jnp.float32)
    lo = drift - hi
    return jnp.where(row < 3, hi, pltpu.roll(lo, 3, 1)), jnp.where(row < 3, pltpu.roll(hi, 4, 1), pltpu.roll(lo, 7, 1))

def pick(table, hot, a8, out_v, k, owner):
    p = jnp.dot(table, hot, preferred_element_type=jnp.float32)
    acc = [jnp.zeros(a8.shape, jnp.float32)] * 3
    rel = [a8 - o for o in owner]
    for t in range(table.shape[0] // 8):
        acc[t % 3] = jnp.where(rel[t % 3] == float(4 * (t // 3)), p[8*t:8*t+8], acc[t % 3])
    for g in range(SB):
        for q in range(3):
            out_v[pl.ds((k + g)*24 + 8*q, 8), :] = acc[q][:, g*LANES:(g+1)*LANES]

def picked(out_v, f):
    return sum([out_v[pl.ds(3*u + f, GCH, stride=24), :] for u in range(8)])

def owners():
    return [((row_iota((8, SB*LANES)) + 8*c) // 6).astype(jnp.float32) for c in range(3)]

def slots_at(i):
    cells = (GCH, LANES)
    return i*GCH*LANES + lax.broadcasted_iota(jnp.int32, cells, 0) * LANES + lax.broadcasted_iota(jnp.int32, cells, 1)

def split(rows):
    return max(rows // GCH // 2, 1)

def vector_shift(shift):
    return [shift[0:1, f:f + 1] for f in range(3)]

def fill_table(tab_v, pieces):
    tab_v[...] = jnp.zeros_like(tab_v)
    for x, piece in enumerate(pieces):
        tab_v[pl.ds(6*x, 6), :] = piece[0:6]
    return tab_v[...].astype(BF)

def by_x(even, odd):
    return [(odd if x % 2 else even)[x // 2] for x in range(EX)]

PER = LANES // LO
PACKED = up(NA // 2, PER) // PER * 8

def packed(rim):
    blocks = []
    for k in range(0, NA // 2, PER):
        group = [rim[g] for g in range(k, min(k + PER, NA // 2))]
        group.append(jnp.zeros((8, LANES - LO * len(group)), jnp.float32))
        blocks.append(jnp.concatenate(group, axis=1))
    return jnp.concatenate(blocks, axis=0)

def unpacked(block):
    return jnp.stack([block[8*(g // PER):8*(g // PER) + 8, LO*(g % PER):LO*(g % PER) + LO] for g in range(NA // 2)])

def fold_kernel(sums, right, left, out, low, high):
    rim = left.shape[0]
    out[...] = sums[...]
    out[0:rim, :] += left[...]
    out[CX * 4:CX * 4 + rim, :] += right[...]
    full = out[...].reshape(NA // 2, 8, NB)
    low[...] = packed(full[:, :, 0:LO])
    high[...] = packed(full[:, :, HI:HI + LO])

def fold(sums, left, right):
    vm = pl.BlockSpec(memory_space=pltpu.VMEM)
    f32 = jnp.float32
    return pl.pallas_call(
        fold_kernel,
        out_shape=(jax.ShapeDtypeStruct(sums.shape, f32), jax.ShapeDtypeStruct((PACKED, LANES), f32), jax.ShapeDtypeStruct((PACKED, LANES), f32)),
        in_specs=[vm, vm, vm],
        out_specs=(vm, vm, vm),
        compiler_params=pltpu.CompilerParams(vmem_limit_bytes=20*1024*1024),
        name="fold",
    )(sums, right, left)

def middle_kernel(shift_v, count, sums, pos_v, rnd_v, base, tab_v, pick_v, a_v, b_v):
    per = GCH * LANES
    lane = lax.broadcasted_iota(jnp.int32, (1, 1, MID[1]), 2)
    pieces = [jnp.where(lane < LO, 0.0, t) for t in drifts(sums[:, :MID[1]].reshape(NA // 2, 8, MID[1]))]
    table = fill_table(tab_v, by_x(*pieces))[:, MID[0]:]
    owner = owners()
    shift = vector_shift(shift_v)
    n = count[0, 0]
    def body(i, c):
        s = pl.ds(pl.multiple_of(i*GCH, GCH), GCH)
        a, b = place(pos_v, s, shift, jnp.int32)
        a_v[...], b_v[...] = a.astype(jnp.float32), b.astype(jnp.float32)
        for k in range(0, GCH, SB):
            hot = hot_tiles(spread(b_v, k, SB, 16).astype(BF), range(MID[0] // 16, MID[1] // 16))
            pick(table, hot, spread(a_v, k, SB, 8), pick_v, k, owner)
        alive = slots_at(i) < n
        for f in range(3):
            base[f, s] = jnp.where(alive, picked(pick_v, f) + rnd_v[f, s], 0.0)
        r = jnp.where(b < LO, b, b - (HI - LO)) + (a & 1) * (2 * LO)
        base[3, s] = (a >> 1).astype(jnp.float32)
        base[4, s] = jnp.where(((b < LO) | (b >= HI)) & alive, r, -1).astype(jnp.float32)
        return c
    lax.fori_loop(0, jnp.minimum((n + (per - 1)) // per, base.shape[1] // GCH), body, 0)

def middle(shift, count, sums, pos, rnd):
    rows = rnd.shape[1]
    part = split(rows) * GCH
    sm = pl.BlockSpec(memory_space=pltpu.SMEM)
    vm = pl.BlockSpec(memory_space=pltpu.VMEM)
    f32 = jnp.float32
    return pl.pallas_call(
        middle_kernel,
        out_shape=jax.ShapeDtypeStruct((5, part, LANES), f32),
        in_specs=[vm, sm, vm, vm, vm],
        out_specs=vm,
        scratch_shapes=[pltpu.VMEM((up(EX*6, 8), MID[1]), f32), pltpu.VMEM((GCH*24, LANES), f32), pltpu.VMEM((GCH, LANES), f32), pltpu.VMEM((GCH, LANES), f32)],
        compiler_params=pltpu.CompilerParams(vmem_limit_bytes=20*1024*1024),
        cost_estimate=pl.CostEstimate(flops=2 * rows * LANES * 128 * 128, bytes_accessed=rows * LANES * 36, transcendentals=0),
        name="middle",
    )(shift, count, sums, pos, rnd)

def last_kernel(shift_v, count, sums, left, right, base, pos_v, rnd_v, out_h, out_v, tab_v, full_v, pick_v, a_v, b_v, osems):
    rows = rnd_v.shape[1]
    per = GCH * LANES
    f32 = jnp.float32
    n = count[0, 0]
    live = (n + (per - 1)) // per
    early = jnp.minimum(live, base.shape[1] // GCH)
    def ocopy(i):
        s = pl.ds(pl.multiple_of(i*GCH, GCH), GCH)
        return pltpu.make_async_copy(out_v.at[:, s], out_h.at[:, s], osems.at[i])
    def dead(i, c):
        out_v[:, pl.ds(pl.multiple_of(i*GCH, GCH), GCH)] = jnp.zeros((3, GCH, LANES), f32)
        ocopy(i).start()
        return c
    lax.fori_loop(live, rows // GCH, dead, 0)
    full = sums[...].reshape(NA // 2, 8, NB)
    low = full[:, :, 0:LO] + unpacked(left[...])
    high = full[:, :, HI:HI + LO] + unpacked(right[...])
    even, odd = drifts(jnp.concatenate([low, high], axis=2))
    table = fill_table(tab_v, jnp.concatenate([even, odd], axis=2))
    owner = owners()
    def body(i, c):
        s = pl.ds(pl.multiple_of(i*GCH, GCH), GCH)
        for k in range(0, GCH, SB):
            hot = hot_tiles(spread(base.at[4], i*GCH + k, SB, 16).astype(BF), range(RK // 16))
            pick(table, hot, spread(base.at[3], i*GCH + k, SB, 8), pick_v, k, owner)
        for f in range(3):
            out_v[f, s] = picked(pick_v, f) + base[f, s]
        ocopy(i).start()
        return c
    lax.fori_loop(0, early, body, 0)
    @pl.when(live > early)
    def _():
        both = jnp.concatenate([low, full[:, :, LO:HI], high, full[:, :, HI + LO:]], axis=2)
        table = fill_table(full_v, by_x(*drifts(both)))
        shift = vector_shift(shift_v)
        def body(i, c):
            s = pl.ds(pl.multiple_of(i*GCH, GCH), GCH)
            a_v[...], b_v[...] = place(pos_v, s, shift)
            for k in range(0, GCH, SB):
                hot = hot_tiles(spread(b_v, k, SB, 16).astype(BF), range(NB // 16))
                pick(table, hot, spread(a_v, k, SB, 8), pick_v, k, owner)
            alive = slots_at(i) < n
            for f in range(3):
                out_v[f, s] = jnp.where(alive, picked(pick_v, f) + rnd_v[f, s], 0.0)
            ocopy(i).start()
            return c
        lax.fori_loop(early, live, body, 0)
    def fin(i, c):
        ocopy(i).wait()
        return c
    lax.fori_loop(0, rows // GCH, fin, 0)

def last(shift, count, sums, left, right, base, pos, rnd):
    rows = rnd.shape[1]
    hbm = pl.BlockSpec(memory_space=pl.ANY)
    sm = pl.BlockSpec(memory_space=pltpu.SMEM)
    vm = pl.BlockSpec(memory_space=pltpu.VMEM)
    f32 = jnp.float32
    return pl.pallas_call(
        last_kernel,
        out_shape=jax.ShapeDtypeStruct((3, rows, LANES), f32),
        in_specs=[vm, sm, vm, vm, vm, vm, vm, vm],
        out_specs=hbm,
        scratch_shapes=[pltpu.VMEM((3, rows, LANES), f32), pltpu.VMEM((up(NA // 2 * 6, 8), RK), f32), pltpu.VMEM((up(EX*6, 8), NB), f32), pltpu.VMEM((GCH*24, LANES), f32),
                        pltpu.VMEM((GCH, LANES), f32), pltpu.VMEM((GCH, LANES), f32), pltpu.SemaphoreType.DMA((rows//GCH,))],
        compiler_params=pltpu.CompilerParams(vmem_limit_bytes=20*1024*1024),
        name="last",
    )(shift, count, sums, left, right, base, pos, rnd)

def shifted(x, axis, step):
    n = lax.axis_size(axis)
    return lax.ppermute(x, axis, [(i, (i + step) % n) for i in range(n)])

def on_device(positions, velocity, random_velocity, masses, counts, grid_shift):
    dense = lambda x: x.reshape(x.shape[-2] if x.ndim == 4 else 1, x.shape[-1] // LANES, LANES)
    pos, vel, rnd, mass = map(dense, (positions, velocity, random_velocity, masses))
    shift = (grid_shift + SKIN * SUB).reshape(1, -1)
    acc = scatter(shift, counts, pos, vel, rnd, mass)
    rim, far = up(RIM * 4, 8), CX * 4
    left = shifted(acc[far:far + rim], "gx", 1)
    right = shifted(acc[0:rim], "gx", -1)
    acc, low, high = fold(acc, left, right)
    left = shifted(high, "gy", 1)
    right = shifted(low, "gy", -1)
    base = middle(shift, counts, acc, pos, rnd)
    out = last(shift, counts, acc, left, right, base, pos, rnd)
    return out.reshape(random_velocity.shape)

def solution(mesh):
    return jax.shard_map(
        on_device, mesh=mesh,
        in_specs=(P("gx", "gy", None, None), P("gx", "gy", None, None), P("gx", "gy", None, None), P("gx", "gy", None), P("gx", "gy"), P()),
        out_specs=P("gx", "gy", None, None), check_vma=False)
```

```python
import functools
import jax, jax.numpy as jnp
from jax import lax
from jax.experimental import pallas as pl
from jax.experimental.pallas import tpu as pltpu
from jax.sharding import PartitionSpec as P

CX = CY = 16; NZ = 8; SKIN = 1; SUB = 16
EX = CX + 2*SKIN + 1; EY = CY + 2*SKIN + 1
LANES = 128
CH = 96
RIM = 2 * SKIN + 1
BF = jnp.bfloat16
SCATTER_VMEM = 55060*1024

def up(x, m): return (x + m - 1) // m * m
NB = up(EY*NZ, 16)
NA = up(EX, 2)

def row_iota(shape): return lax.broadcasted_iota(jnp.int32, shape, len(shape) - 2)

def spread(ref, base, count, sublanes):
    return jnp.concatenate([jnp.broadcast_to(ref[pl.ds(base + g, 1), :], (sublanes, LANES)) for g in range(count)], axis=1)

def place(pos_v, s, shift, kind=jnp.float32):
    a = ((pos_v[0, s] + shift[0]) >> 4)
    b = (((pos_v[1, s] + shift[1]) >> 4)) * NZ + (((pos_v[2, s] + shift[2]) >> 4) & (NZ - 1))
    return a.astype(kind), b.astype(kind)

def load_shift(shift_h, shift, sem):
    copy = pltpu.make_async_copy(shift_h, shift, sem)
    copy.start()
    return copy

def scatter_kernel(shift_h, count, pos_h, vel_h, rnd_h, mass_h, out, acc, pos_v, vel_v, rnd_v, mass_v, val_v, a_v, b_v, shift, ssem, sems):
    shift_copy = load_shift(shift_h, shift, ssem)
    per = CH * LANES
    def copies(i):
        s = pl.ds(pl.multiple_of(i*CH, CH), CH)
        return [pltpu.make_async_copy(h.at[:, s], v.at[:, s], sems.at[i]) for h, v in
                ((pos_h, pos_v), (vel_h, vel_v), (rnd_h, rnd_v), (mass_h, mass_v))]
    def start(i, c):
        for x in copies(i): x.start()
        return c
    start(0, 0)
    acc[...] = jnp.zeros_like(acc)
    shift_copy.wait()
    moved = [shift[0, f] for f in range(3)]
    n = count[0, 0]
    live = (n + (per - 1)) // per
    lax.fori_loop(1, live, start, 0)
    slot = lax.broadcasted_iota(jnp.int32, (CH, LANES), 0) * LANES + lax.broadcasted_iota(jnp.int32, (CH, LANES), 1)
    def body(i, c):
        for x in copies(i): x.wait()
        base = pl.multiple_of(i*CH, CH)
        s = pl.ds(base, CH)
        a_v[...], b_v[...] = place(pos_v, s, moved)
        w = jnp.where(slot + i*per < n, mass_v[0, s], 0.0)
        fields = [(vel_v[f, s] - rnd_v[f, s]) * w for f in range(3)] + [w]
        for f, x in enumerate(fields):
            hi = x.astype(BF).astype(jnp.float32)
            val_v[pl.ds(f, CH, stride=8), :] = hi
            val_v[pl.ds(f + 4, CH, stride=8), :] = x - hi
        b16 = spread(b_v, 0, CH, 16).astype(BF)
        rhs = hot_tiles(b16, range(NB // 16))
        a16 = spread(a_v, 0, CH, 16).astype(BF)
        width = CH * LANES
        rel = a16 - (row_iota((16, width)) >> 3).astype(jnp.float32).astype(BF)
        v8 = [val_v[pl.ds(8*g, 8), :] for g in range(CH)]
        v16 = jnp.concatenate([jnp.concatenate([x, x], axis=0) for x in v8], axis=1).astype(BF)
        zero = jnp.zeros((16, width), BF)
        lhs = jnp.concatenate([jnp.where(rel == BF(2*t), v16, zero) for t in range(NA // 2)], axis=0)
        acc[...] += lax.dot_general(lhs, rhs, (((1,), (1,)), ((), ())), preferred_element_type=jnp.float32)
        return c
    lax.fori_loop(0, live, body, 0)
    both = acc[...].reshape(NA // 2, 2, 8, NB)
    both = both + pltpu.roll(both.reshape(NA, 8, NB), 4, 1).reshape(both.shape)
    out[...] = jnp.where(row_iota((1, 8, NB)) < 4, both[:, 0], both[:, 1]).reshape(NA * 4, NB)

def scatter(shift, count, pos, vel, rnd, mass):
    rows = pos.shape[1]
    hbm = pl.BlockSpec(memory_space=pl.ANY)
    sm = pl.BlockSpec(memory_space=pltpu.SMEM)
    vm = pl.BlockSpec(memory_space=pltpu.VMEM)
    f32 = jnp.float32
    return pl.pallas_call(
        scatter_kernel,
        out_shape=jax.ShapeDtypeStruct((NA*4, NB), f32),
        in_specs=[hbm, sm, hbm, hbm, hbm, hbm],
        out_specs=vm,
        scratch_shapes=[pltpu.VMEM((NA*8, NB), f32), pltpu.VMEM((3, rows, LANES), jnp.int32), pltpu.VMEM((3, rows, LANES), f32), pltpu.VMEM((3, rows, LANES), f32),
                        pltpu.VMEM((1, rows, LANES), f32), pltpu.VMEM((CH * 8 + 8, LANES), f32), pltpu.VMEM((CH, LANES), f32), pltpu.VMEM((CH, LANES), f32),
                        pltpu.SMEM(shift.shape, jnp.int32), pltpu.SemaphoreType.DMA(()), pltpu.SemaphoreType.DMA((rows // CH,))],
        compiler_params=pltpu.CompilerParams(vmem_limit_bytes=SCATTER_VMEM),
        name="scatter",
    )(shift, count, pos, vel, rnd, mass)

SB = 4
LO = RIM * NZ
HI = CY * NZ
MID = (LO // 16 * 16, HI)
RK = 2 * 2 * LO
GCH = 192
OCH = 64
PARTS = GCH // OCH

def hot_tiles(b16, tiles):
    width = b16.shape[1]
    rel = b16 - row_iota((16, width)).astype(jnp.float32).astype(BF)
    one, zero = jnp.ones((16, width), BF), jnp.zeros((16, width), BF)
    return jnp.concatenate([jnp.where(rel == BF(16*t), one, zero) for t in tiles], axis=0)

def drifts(sums):
    row = row_iota((1,) + sums.shape[1:])
    mass = jnp.where(row < 4, sums[:, 3:4], sums[:, 7:8])
    filled = mass > 0
    drift = jnp.where(filled, sums / jnp.where(filled, mass, 1.0), 0.0)
    hi = drift.astype(BF).astype(jnp.float32)
    lo = drift - hi
    return jnp.where(row < 3, hi, pltpu.roll(lo, 3, 1)), jnp.where(row < 3, pltpu.roll(hi, 4, 1), pltpu.roll(lo, 7, 1))

def pick(table, hot, a8, out_v, k, owner):
    p = jnp.dot(table, hot, preferred_element_type=jnp.float32)
    acc = [jnp.zeros(a8.shape, jnp.float32)] * 3
    rel = [a8 - o for o in owner]
    for t in range(table.shape[0] // 8):
        acc[t % 3] = jnp.where(rel[t % 3] == float(4 * (t // 3)), p[8*t:8*t+8], acc[t % 3])
    for g in range(SB):
        for q in range(3):
            out_v[pl.ds((k + g)*24 + 8*q, 8), :] = acc[q][:, g*LANES:(g+1)*LANES]

def picked(out_v, f, start=0, count=GCH):
    return sum([out_v[pl.ds(24*start + 3*u + f, count, stride=24), :] for u in range(8)])

def owners():
    return [((row_iota((8, SB*LANES)) + 8*c) // 6).astype(jnp.float32) for c in range(3)]

def slots_at(i):
    cells = (GCH, LANES)
    return i*GCH*LANES + lax.broadcasted_iota(jnp.int32, cells, 0) * LANES + lax.broadcasted_iota(jnp.int32, cells, 1)

def split(rows):
    return max(rows // GCH // 2, 1)

def vector_shift(shift):
    return [shift[0:1, f:f + 1] for f in range(3)]

def fill_table(tab_v, pieces):
    tab_v[...] = jnp.zeros_like(tab_v)
    for x, piece in enumerate(pieces):
        tab_v[pl.ds(6*x, 6), :] = piece[0:6]
    return tab_v[...].astype(BF)

def by_x(even, odd):
    return [(odd if x % 2 else even)[x // 2] for x in range(EX)]

PER = LANES // LO
PACKED = up(NA // 2, PER) // PER * 8

def packed(rim):
    blocks = []
    for k in range(0, NA // 2, PER):
        group = [rim[g] for g in range(k, min(k + PER, NA // 2))]
        group.append(jnp.zeros((8, LANES - LO * len(group)), jnp.float32))
        blocks.append(jnp.concatenate(group, axis=1))
    return jnp.concatenate(blocks, axis=0)

def unpacked(block):
    return jnp.stack([block[8*(g // PER):8*(g // PER) + 8, LO*(g % PER):LO*(g % PER) + LO] for g in range(NA // 2)])

def fold_kernel(sums, right, left, out, low, high):
    rim = left.shape[0]
    out[...] = sums[...]
    out[0:rim, :] += left[...]
    out[CX * 4:CX * 4 + rim, :] += right[...]
    full = out[...].reshape(NA // 2, 8, NB)
    low[...] = packed(full[:, :, 0:LO])
    high[...] = packed(full[:, :, HI:HI + LO])

def fold(sums, left, right):
    vm = pl.BlockSpec(memory_space=pltpu.VMEM)
    f32 = jnp.float32
    return pl.pallas_call(
        fold_kernel,
        out_shape=(jax.ShapeDtypeStruct(sums.shape, f32), jax.ShapeDtypeStruct((PACKED, LANES), f32), jax.ShapeDtypeStruct((PACKED, LANES), f32)),
        in_specs=[vm, vm, vm],
        out_specs=(vm, vm, vm),
        compiler_params=pltpu.CompilerParams(vmem_limit_bytes=20*1024*1024),
        name="fold",
    )(sums, right, left)

def middle_kernel(shift_v, count, sums, pos_v, rnd_v, base, tab_v, pick_v, a_v, b_v):
    per = GCH * LANES
    lane = lax.broadcasted_iota(jnp.int32, (1, 1, MID[1]), 2)
    pieces = [jnp.where(lane < LO, 0.0, t) for t in drifts(sums[:, :MID[1]].reshape(NA // 2, 8, MID[1]))]
    table = fill_table(tab_v, by_x(*pieces))[:, MID[0]:]
    owner = owners()
    shift = vector_shift(shift_v)
    n = count[0, 0]
    def body(i, c):
        s = pl.ds(pl.multiple_of(i*GCH, GCH), GCH)
        a, b = place(pos_v, s, shift, jnp.int32)
        a_v[...], b_v[...] = a.astype(jnp.float32), b.astype(jnp.float32)
        for k in range(0, GCH, SB):
            hot = hot_tiles(spread(b_v, k, SB, 16).astype(BF), range(MID[0] // 16, MID[1] // 16))
            pick(table, hot, spread(a_v, k, SB, 8), pick_v, k, owner)
        alive = slots_at(i) < n
        for f in range(3):
            base[f, s] = jnp.where(alive, picked(pick_v, f) + rnd_v[f, s], 0.0)
        r = jnp.where(b < LO, b, b - (HI - LO)) + (a & 1) * (2 * LO)
        base[3, s] = (a >> 1).astype(jnp.float32)
        base[4, s] = jnp.where(((b < LO) | (b >= HI)) & alive, r, -1).astype(jnp.float32)
        return c
    lax.fori_loop(0, jnp.minimum((n + (per - 1)) // per, base.shape[1] // GCH), body, 0)

def middle(shift, count, sums, pos, rnd):
    rows = rnd.shape[1]
    part = split(rows) * GCH
    sm = pl.BlockSpec(memory_space=pltpu.SMEM)
    vm = pl.BlockSpec(memory_space=pltpu.VMEM)
    f32 = jnp.float32
    return pl.pallas_call(
        middle_kernel,
        out_shape=jax.ShapeDtypeStruct((5, part, LANES), f32),
        in_specs=[vm, sm, vm, vm, vm],
        out_specs=vm,
        scratch_shapes=[pltpu.VMEM((up(EX*6, 8), MID[1]), f32), pltpu.VMEM((GCH*24 + 24, LANES), f32), pltpu.VMEM((GCH, LANES), f32), pltpu.VMEM((GCH, LANES), f32)],
        compiler_params=pltpu.CompilerParams(vmem_limit_bytes=20*1024*1024),
        cost_estimate=pl.CostEstimate(flops=2 * rows * LANES * 128 * 128, bytes_accessed=rows * LANES * 36, transcendentals=0),
        name="middle",
    )(shift, count, sums, pos, rnd)

def last_kernel(shift_v, count, sums, left, right, base, pos_v, rnd_v, out_h, out_v, tab_v, full_v, pick_v, a_v, b_v, osems):
    rows = rnd_v.shape[1]
    per = GCH * LANES
    f32 = jnp.float32
    n = count[0, 0]
    live = (n + (per - 1)) // per
    early = jnp.minimum(live, base.shape[1] // GCH)
    def ocopy(i):
        s = pl.ds(pl.multiple_of(i*OCH, OCH), OCH)
        return pltpu.make_async_copy(out_v.at[:, s], out_h.at[:, s], osems.at[i])
    def dead(i, c):
        out_v[:, pl.ds(pl.multiple_of(i*OCH, OCH), OCH)] = jnp.zeros((3, OCH, LANES), f32)
        ocopy(i).start()
        return c
    lax.fori_loop(live * PARTS, rows // OCH, dead, 0)
    full = sums[...].reshape(NA // 2, 8, NB)
    low = full[:, :, 0:LO] + unpacked(left[...])
    high = full[:, :, HI:HI + LO] + unpacked(right[...])
    even, odd = drifts(jnp.concatenate([low, high], axis=2))
    table = fill_table(tab_v, jnp.concatenate([even, odd], axis=2))
    owner = owners()
    def body(i, c):
        for part in range(PARTS):
            for k in range(part*OCH, part*OCH + OCH, SB):
                hot = hot_tiles(spread(base.at[4], i*GCH + k, SB, 16).astype(BF), range(RK // 16))
                pick(table, hot, spread(base.at[3], i*GCH + k, SB, 8), pick_v, k, owner)
            s = pl.ds(pl.multiple_of(i*GCH + part*OCH, OCH), OCH)
            for f in range(3):
                out_v[f, s] = picked(pick_v, f, part*OCH, OCH) + base[f, s]
            ocopy(i*PARTS + part).start()
        return c
    lax.fori_loop(0, early, body, 0)
    @pl.when(live > early)
    def _():
        both = jnp.concatenate([low, full[:, :, LO:HI], high, full[:, :, HI + LO:]], axis=2)
        table = fill_table(full_v, by_x(*drifts(both)))
        shift = vector_shift(shift_v)
        def body(i, c):
            s = pl.ds(pl.multiple_of(i*GCH, GCH), GCH)
            a_v[...], b_v[...] = place(pos_v, s, shift)
            for part in range(PARTS):
                for k in range(part*OCH, part*OCH + OCH, SB):
                    hot = hot_tiles(spread(b_v, k, SB, 16).astype(BF), range(NB // 16))
                    pick(table, hot, spread(a_v, k, SB, 8), pick_v, k, owner)
                s = pl.ds(pl.multiple_of(i*GCH + part*OCH, OCH), OCH)
                alive = slots_at(i)[part*OCH:part*OCH + OCH] < n
                for f in range(3):
                    out_v[f, s] = jnp.where(alive, picked(pick_v, f, part*OCH, OCH) + rnd_v[f, s], 0.0)
                ocopy(i*PARTS + part).start()
            return c
        lax.fori_loop(early, live, body, 0)
    def fin(i, c):
        ocopy(i).wait()
        return c
    lax.fori_loop(0, rows // OCH, fin, 0)

def last(shift, count, sums, left, right, base, pos, rnd):
    rows = rnd.shape[1]
    hbm = pl.BlockSpec(memory_space=pl.ANY)
    sm = pl.BlockSpec(memory_space=pltpu.SMEM)
    vm = pl.BlockSpec(memory_space=pltpu.VMEM)
    f32 = jnp.float32
    return pl.pallas_call(
        last_kernel,
        out_shape=jax.ShapeDtypeStruct((3, rows, LANES), f32),
        in_specs=[vm, sm, vm, vm, vm, vm, vm, vm],
        out_specs=hbm,
        scratch_shapes=[pltpu.VMEM((3, rows, LANES), f32), pltpu.VMEM((up(NA // 2 * 6, 8), RK), f32), pltpu.VMEM((up(EX*6, 8), NB), f32), pltpu.VMEM((GCH*24 + 24, LANES), f32),
                        pltpu.VMEM((GCH, LANES), f32), pltpu.VMEM((GCH, LANES), f32), pltpu.SemaphoreType.DMA((rows//OCH,))],
        compiler_params=pltpu.CompilerParams(vmem_limit_bytes=20*1024*1024),
        name="last",
    )(shift, count, sums, left, right, base, pos, rnd)

def shifted(x, axis, step):
    n = lax.axis_size(axis)
    return lax.ppermute(x, axis, [(i, (i + step) % n) for i in range(n)])

def on_device(positions, velocity, random_velocity, masses, counts, grid_shift):
    dense = lambda x: x.reshape(x.shape[-2] if x.ndim == 4 else 1, x.shape[-1] // LANES, LANES)
    pos, vel, rnd, mass = map(dense, (positions, velocity, random_velocity, masses))
    shift = (grid_shift + SKIN * SUB).reshape(1, -1)
    acc = scatter(shift, counts, pos, vel, rnd, mass)
    rim, far = up(RIM * 4, 8), CX * 4
    left = shifted(acc[far:far + rim], "gx", 1)
    right = shifted(acc[0:rim], "gx", -1)
    acc, low, high = fold(acc, left, right)
    left = shifted(high, "gy", 1)
    right = shifted(low, "gy", -1)
    base = middle(shift, counts, acc, pos, rnd)
    out = last(shift, counts, acc, left, right, base, pos, rnd)
    return out.reshape(random_velocity.shape)

def solution(mesh):
    return jax.shard_map(
        on_device, mesh=mesh,
        in_specs=(P("gx", "gy", None, None), P("gx", "gy", None, None), P("gx", "gy", None, None), P("gx", "gy", None), P("gx", "gy"), P()),
        out_specs=P("gx", "gy", None, None), check_vma=False)
```
